512 devices in a mesh: gx: 32 (over z_lo, y), gy: 8 (over x, core), gz: 2 (over z_hi).
Axes of the slice: x: 4, y: 4, z: 16 (z_hi: 2, z_lo: 8; z = z_hi * 8 + z_lo), core: 2. Of those that a mesh axis runs over, the one named last changes fastest.
Arguments:
- features: bfloat16 [32, 8, 2, 128, 256], P('gx', 'gy', 'gz'), may hold values from -6 to 6
- positions: bfloat16 [32, 8, 2, 3, 128], P('gx', 'gy', 'gz'), may hold values from 0 to 8
- neighbours: int32 [32, 8, 2, 12, 128], P('gx', 'gy', 'gz'), may hold values from 0 to 3455
- counts: int32 [32, 8, 2, 128], P('gx', 'gy', 'gz'), may hold values from 3 to 12
- cell_index: int32 [32, 8, 2, 3, 64, 128], P('gx', 'gy', 'gz'), may hold values from 0 to 133, as said below
- spline_weight: float32 [32, 8, 2, 64, 128], P('gx', 'gy', 'gz'), may hold values from 0 to 1
- spline_slope: float32 [32, 8, 2, 3, 64, 128], P('gx', 'gy', 'gz'), may hold values from -4 to 4
- radial_in: float32 [8, 64], replicated, may hold values from -4 to 4
- radial_out: float32 [64, 192], replicated, may hold values from -0.75 to 0.75
- mix_scalar: bfloat16 [64, 64], replicated, may hold values from -1.5 to 1.5
- mix_vector: bfloat16 [64, 64], replicated, may hold values from -1.5 to 1.5
- mix_gate: bfloat16 [64, 64], replicated, may hold values from -1.5 to 1.5
- charge_head: float32 [64], replicated, may hold values from -0.75 to 0.75
Outputs:
- updated: bfloat16 [32, 8, 2, 128, 256], P('gx', 'gy', 'gz')
- forces: float32 [32, 8, 2, 3, 128], P('gx', 'gy', 'gz')
The draws below stay inside these ranges and needn't reach their ends.
Inputs may be any that keep to these rules, and one draw needn't show every extreme that they name: `cell_index`: coordinate 0 lies below 8 + 6, coordinate 1 below 32 + 6, coordinate 2 below 128 + 6.
All inputs are finite; a program needn't handle non-finite values.
Results may differ from the reference program's by a relative error of at most 0.015.
Values may be sent and summed in bfloat16 or wider, within the bound.
A program may use at most 64 MiB of HBM per device.

```python
import math
import jax
import jax.numpy as jnp
from jax import lax

MESH = 256
ATOMS = 128
NEIGH = 12
CHAN = 64
RADIAL = 64
BASIS = 8
SPLINE = 64
MX = 8
MY = 32
MZ = 128
N_GX = 32
N_GY = 8
N_GZ = 2


def draw_cell_index(key, part):
    key = jax.random.fold_in(key, 11)
    limits = jnp.array([MX + 6, MY + 6, MZ + 6], dtype=jnp.int32)
    drawn = jax.random.randint(key, (N_GX, N_GY, N_GZ, 3, SPLINE, ATOMS), 0, limits[:, None, None])
    drawn = drawn.at[:, :, :, :, 0, 0].set(jnp.broadcast_to(limits - 1, (N_GX, N_GY, N_GZ, 3)))
    drawn = drawn.at[:, :, :, :, 1, 0].set(0)
    return drawn.astype(jnp.int32)


def place_ends(values, rng, least, top_value):
    longest = values.shape.index(max(values.shape))
    spots = []
    for shift in (0, 1):
        where = [jax.random.randint(jax.random.fold_in(rng, axis), (), 0, length) for axis, length in enumerate(values.shape)]
        where[longest] = (where[longest] + shift) % values.shape[longest]
        spots.append(tuple(where))
    return values.at[spots[0]].set(least).at[spots[1]].set(top_value)


def levels(key, extent, shards, least, top_value):
    def one(position, blocks):
        heights = jax.random.uniform(jax.random.fold_in(jax.random.fold_in(key, 6), position), (blocks,), jnp.float32, least / len(shards), top_value / len(shards))
        return jnp.repeat(jnp.exp(heights), extent[position] // blocks).reshape((-1,) + (1,) * (len(extent) - position - 1))

    loudness = one(*shards[0])
    for cut in shards[1:]:
        loudness = loudness * one(*cut)
    return loudness


def normal_values(key, shape, width, limit, shards=(), held_as=jnp.bfloat16):
    entries = jax.random.normal(key, shape, jnp.float32) * width
    if len(shards) > 0:
        entries = levels(key, shape, shards, -0.22, 0.18) * entries
    return jnp.clip(entries, min=-limit, max=limit).astype(held_as)


def setup_inputs(seed: int = 0) -> dict:
    key_list = jax.random.split(jax.random.key(seed), 14)
    return {
        "features": normal_values(key_list[0], (N_GX, N_GY, N_GZ, ATOMS, 4 * CHAN), 1.0, 6.0, ((0, 32), (1, 8), (2, 2))),
        "positions": jnp.clip(8.0 * jax.random.uniform(key_list[1], (N_GX, N_GY, N_GZ, 3, ATOMS), jnp.float32) ** levels(key_list[1], (N_GX, N_GY, N_GZ, 3, ATOMS), ((0, 32), (1, 8), (2, 2)), -0.2, 0.2), 0.0, 8.0).astype(jnp.bfloat16),
        "neighbours": place_ends(jax.random.randint(key_list[2], (N_GX, N_GY, N_GZ, NEIGH, ATOMS), 0, 27 * ATOMS), jax.random.fold_in(key_list[2], 1), 0, (27 * ATOMS) - 1).astype(jnp.int32),
        "counts": place_ends(jax.random.randint(key_list[3], (N_GX, N_GY, N_GZ, ATOMS), NEIGH // 4, NEIGH + 1), jax.random.fold_in(key_list[3], 1), NEIGH // 4, NEIGH).astype(jnp.int32),
        "cell_index": draw_cell_index(jax.random.fold_in(key_list[13], 71), 0),
        "spline_weight": jnp.clip(1.0 * jax.random.uniform(key_list[5], (N_GX, N_GY, N_GZ, SPLINE, ATOMS), jnp.float32) ** levels(key_list[5], (N_GX, N_GY, N_GZ, SPLINE, ATOMS), ((0, 32), (1, 8), (2, 2)), -0.2, 0.2), 0.0, 1.0),
        "spline_slope": normal_values(key_list[6], (N_GX, N_GY, N_GZ, 3, SPLINE, ATOMS), 0.5, 4.0, ((0, 32), (1, 8), (2, 2)), jnp.float32),
        "radial_in": normal_values(key_list[7], (BASIS, RADIAL), 2 ** -0.5, 4.0, (), jnp.float32),
        "radial_out": normal_values(key_list[8], (RADIAL, 3 * CHAN), RADIAL ** -0.5, 0.75, (), jnp.float32),
        "mix_scalar": normal_values(key_list[9], (CHAN, CHAN), (CHAN // 4) ** -0.5, 1.5),
        "mix_vector": normal_values(key_list[10], (CHAN, CHAN), (CHAN // 4) ** -0.5, 1.5),
        "mix_gate": normal_values(key_list[11], (CHAN, CHAN), (CHAN // 4) ** -0.5, 1.5),
        "charge_head": normal_values(key_list[12], (CHAN,), CHAN ** -0.5, 0.75, (), jnp.float32),
    }


box_side = 8.0
highest = lax.Precision.HIGHEST

def atom_layer(table_feat, table_pos, own_feat, own_pos, nbr_rows, nbr_count, radial_in, radial_out, mix_scalar, mix_vector, mix_gate, charge_head):
    chan_count = own_feat.shape[1] // 4
    edge_count, atom_count = nbr_rows.shape
    flat_rows = nbr_rows.reshape(-1)
    picked = jnp.take(table_feat, flat_rows, axis=0).astype(jnp.float32).reshape(edge_count, atom_count, 4 * chan_count)
    others = jnp.take(table_pos, flat_rows, axis=1).reshape(3, edge_count, atom_count)
    delta = others - own_pos[:, None, :]
    length = jnp.sqrt(lax.optimization_barrier(jnp.sum(delta * delta, axis=0)) + 1.0)
    direction = jnp.transpose(delta / length, (1, 2, 0))
    centres = 4.0 * jnp.arange(radial_in.shape[0], dtype=jnp.float32)
    basis = jnp.exp(-jnp.square(length[:, :, None] - centres) / 8.0)
    hidden = jax.nn.silu(jnp.einsum('kan,nh->kah', basis, radial_in, precision=highest))
    radial = jnp.einsum('kah,hc->kac', hidden, radial_out, precision=highest)
    radial_zero = radial[..., :chan_count]
    radial_one = radial[..., chan_count:2 * chan_count]
    radial_two = radial[..., 2 * chan_count:]
    scalars = picked[..., :chan_count]
    vectors = picked[..., chan_count:].reshape(edge_count, atom_count, 3, chan_count)
    along = lax.optimization_barrier(jnp.sum(direction[..., None] * vectors, axis=2))
    live = (jnp.arange(edge_count, dtype=jnp.int32)[:, None] < nbr_count[None, :]).astype(jnp.float32)[..., None]
    message_s = (radial_zero * scalars + radial_two * along) * live
    message_v = ((radial_one * scalars)[:, :, None, :] * direction[..., None] + radial_two[:, :, None, :] * vectors) * live[:, :, None, :]
    agg_s = (lax.optimization_barrier(jnp.sum(message_s, axis=0)) / edge_count).astype(jnp.bfloat16)
    agg_v = (lax.optimization_barrier(jnp.sum(message_v, axis=0)) / edge_count).astype(jnp.bfloat16)
    mixed_s = jnp.dot(agg_s, mix_scalar, preferred_element_type=jnp.float32)
    gating = jax.nn.sigmoid(jnp.dot(agg_s, mix_gate, preferred_element_type=jnp.float32))
    mixed_v = jnp.dot(agg_v.reshape(atom_count * 3, chan_count), mix_vector, preferred_element_type=jnp.float32).reshape(atom_count, 3, chan_count)
    own_values = own_feat.astype(jnp.float32)
    new_s = own_values[:, :chan_count] + jax.nn.silu(mixed_s)
    new_v = own_values[:, chan_count:].reshape(atom_count, 3, chan_count) + mixed_v * gating[:, None, :]
    result = jnp.concatenate([new_s, new_v.reshape(atom_count, 3 * chan_count)], axis=1).astype(jnp.bfloat16)
    charge = jnp.dot(result[:, :chan_count].astype(jnp.float32), charge_head, precision=highest)
    return (result, charge)

def green_values(freq_x, freq_y, freq_z, mesh_cells):

    def signed(index):
        return jnp.where(2 * index < mesh_cells, index, index - mesh_cells).astype(jnp.float32)
    step_size = 2.0 * math.pi / mesh_cells
    ksquare = step_size * step_size * (jnp.square(signed(freq_x)) + jnp.square(signed(freq_y)) + jnp.square(signed(freq_z)))
    screen = 4.0 * math.pi / mesh_cells
    value = jnp.exp(-0.5 * ksquare) / (ksquare + screen * screen)
    anchor = (freq_x == 0) & (freq_y == 0) & (freq_z == 0)
    return jnp.where(anchor, jnp.zeros_like(value), value)

def reference(features, positions, neighbours, counts, cell_index, spline_weight, spline_slope, radial_in, radial_out, mix_scalar, mix_vector, mix_gate, charge_head):
    grid_x, grid_y, grid_z = (N_GX, N_GY, N_GZ)

    def one_domain(domain):
        pos_x = domain // (grid_y * grid_z)
        pos_y = domain // grid_z % grid_y
        pos_z = domain % grid_z
        feat_list = []
        place_list = []
        for shift_x in (-1, 0, 1):
            for shift_y in (-1, 0, 1):
                for shift_z in (-1, 0, 1):
                    other_x = (pos_x + shift_x) % grid_x
                    other_y = (pos_y + shift_y) % grid_y
                    other_z = (pos_z + shift_z) % grid_z
                    feat_list.append(features[other_x, other_y, other_z])
                    offset = jnp.array([shift_x, shift_y, shift_z], dtype=jnp.float32) * box_side
                    place_list.append(positions[other_x, other_y, other_z].astype(jnp.float32) + offset[:, None])
        table_feat = jnp.concatenate(feat_list, axis=0)
        table_pos = jnp.concatenate(place_list, axis=1)
        return atom_layer(table_feat, table_pos, features[pos_x, pos_y, pos_z], positions[pos_x, pos_y, pos_z].astype(jnp.float32), neighbours[pos_x, pos_y, pos_z], counts[pos_x, pos_y, pos_z], radial_in, radial_out, mix_scalar, mix_vector, mix_gate, charge_head)
    flat_result, flat_charge = lax.map(one_domain, jnp.arange(grid_x * grid_y * grid_z, dtype=jnp.int32))
    updated = flat_result.reshape(features.shape)
    charge = flat_charge.reshape(grid_x, grid_y, grid_z, -1)
    block_x, block_y, block_z = (MESH // grid_x, MESH // grid_y, MESH // grid_z)
    local_x = cell_index[:, :, :, 0]
    local_y = cell_index[:, :, :, 1]
    local_z = cell_index[:, :, :, 2]
    domain_x = jnp.arange(grid_x, dtype=jnp.int32)[:, None, None, None, None]
    domain_y = jnp.arange(grid_y, dtype=jnp.int32)[None, :, None, None, None]
    domain_z = jnp.arange(grid_z, dtype=jnp.int32)[None, None, :, None, None]
    global_x = (domain_x * block_x + local_x - 3) % MESH
    global_y = (domain_y * block_y + local_y - 3) % MESH
    global_z = (domain_z * block_z + local_z - 3) % MESH
    flat_cell = (global_x * MESH + global_y) * MESH + global_z
    spread = (charge[:, :, :, None, :] * spline_weight).reshape(-1)
    density = jnp.zeros((MESH * MESH * MESH,), jnp.float32).at[flat_cell.reshape(-1)].add(spread)
    spectrum = jnp.fft.fftn(density.reshape(MESH, MESH, MESH))
    freq = jnp.arange(MESH, dtype=jnp.int32)
    green = green_values(freq[:, None, None], freq[None, :, None], freq[None, None, :], MESH)
    potential = jnp.real(jnp.fft.ifftn(spectrum * green)).astype(jnp.float32)
    values = potential.reshape(-1)[flat_cell]
    forces = -charge[:, :, :, None, :] * lax.optimization_barrier(jnp.sum(spline_slope * values[:, :, :, None, :, :], axis=4))
    return (updated, forces)
```

```python
import math

import jax
import jax.numpy as jnp
import numpy as np
from jax import lax
from jax.experimental import pallas as pl
from jax.experimental.pallas import tpu as pltpu
from jax.sharding import PartitionSpec as P

MESH = 256
GX, GY, GZ = 32, 8, 2
ATOMS, NEIGH, CHAN, SPLINE = 128, 12, 64, 64
F32, BF16, I32 = jnp.float32, jnp.bfloat16, jnp.int32
BY_MESH = pl.DeviceIdType.MESH
HIGHEST = lax.Precision.HIGHEST
VMEM = pl.BlockSpec(memory_space=pltpu.VMEM)
PLANES = tuple((da, db) for da in (-1, 0, 1) for db in (-1, 0, 1) if (da, db) != (0, 0))
ZPAD = 136
ROWS = 640


def real_basis():
    n = np.arange(MESH)[:, None]
    m = np.arange(MESH)[None, :]
    freq = np.where(m <= 128, m, m - 128)
    angle = 2.0 * np.pi * ((n * freq) % MESH) / MESH
    basis = np.where(m <= 128, np.cos(angle), np.sin(angle)) * np.sqrt(2.0 / MESH)
    basis[:, 0] = 1.0 / np.sqrt(MESH)
    basis[:, 128] /= np.sqrt(2.0)
    return basis


def tables():
    basis = real_basis()
    along_z = np.zeros((GZ, ZPAD, MESH))
    for c in range(GZ):
        along_z[c, :134] = basis[(128 * c + np.arange(134) - 3) % MESH]
    along_y = np.zeros((GY, 128, 3, MESH))
    for b in range(GY):
        for third in range(3):
            along_y[b, third * 40 : third * 40 + 38, third] = basis[
                (32 * b + np.arange(38) - 3) % MESH
            ]
    along_x = np.zeros((GX, 16, MESH))
    for a in range(GX):
        along_x[a, :14] = basis[(8 * a + np.arange(14) - 3) % MESH]
    order = np.zeros((16, 16, 3, 5, 16))
    for p in range(14):
        for k in range(16):
            order[k, p, p % 3, p // 3, k] = 1.0
    as_bf16 = lambda x: jnp.asarray(x, BF16)
    along_x = along_x.reshape(512, 256)
    order = order.reshape(256, 240)
    return dict(
        z_fwd=as_bf16(along_z.transpose(0, 2, 1)),
        z_inv=as_bf16(along_z),
        y=as_bf16(along_y.reshape(1024, 768)),
        x_fwd=as_bf16(along_x.T),
        x_inv=as_bf16(along_x),
        order=as_bf16(order),
        back=as_bf16(order.T),
    )


def dot_nn(a, b, precision=None):
    return jnp.dot(a, b, preferred_element_type=F32, precision=precision)


def dot_nt(a, b):
    return lax.dot_general(a, b, (((1,), (1,)), ((), ())), preferred_element_type=F32)


def silu(x):
    return x / (1.0 + jnp.exp(-x))


def split_rows(rows):
    block = rows >> 7
    slot = rows & 127
    ninth = (block * 43) >> 7
    oz = block - 3 * ninth - 1
    third = (ninth * 43) >> 7
    ox = third - 1
    oy = ninth - 3 * third - 1
    return ninth * 128 + slot, ox, oy, oz


def edge_sums(table, rows, counts, own_pos, same_layer, rin, rout):
    index, ox, oy, oz = split_rows(rows)
    slot = lax.broadcasted_iota(I32, (NEIGH, ATOMS), 0)
    use = (oz == 0) if same_layer else (oz != 0)
    index = jnp.where(use & (slot < counts), index, -1)
    shift = [8.0 * o.astype(F32) for o in (ox, oy, oz)]
    sums = [jnp.zeros((CHAN, 2 * ATOMS), F32) for _ in range(4)]
    rows_iota = lax.broadcasted_iota(I32, (9 * ATOMS, ATOMS), 0)
    centre = 4.0 * lax.broadcasted_iota(I32, (8, 2 * ATOMS), 0).astype(F32)
    for pair in range(NEIGH // 2):
        ks = (2 * pair, 2 * pair + 1)
        pick = jnp.concatenate(
            [jnp.where(rows_iota == index[k : k + 1], 1.0, 0.0).astype(BF16) for k in ks], axis=1
        )
        got = dot_nn(table, pick)
        delta = []
        for d in range(3):
            moved = jnp.concatenate(
                [shift[d][k : k + 1] - own_pos[d : d + 1] for k in ks], axis=1
            )
            delta.append(got[256 + d : 257 + d] + moved)
        length = jnp.sqrt(delta[0] * delta[0] + delta[1] * delta[1] + delta[2] * delta[2] + 1.0)
        unit = [d / length for d in delta]
        off = length - centre
        basis = jnp.exp(off * off * -0.125)
        hidden = silu(dot_nn(rin, basis, HIGHEST))
        radial = dot_nn(rout, hidden, HIGHEST)
        r0, r1, r2 = radial[:CHAN], radial[CHAN : 2 * CHAN], radial[2 * CHAN :]
        s = got[:CHAN]
        v = [got[CHAN * (d + 1) : CHAN * (d + 2)] for d in range(3)]
        along = unit[0] * v[0] + unit[1] * v[1] + unit[2] * v[2]
        sums[0] = sums[0] + (r0 * s + r2 * along)
        turned = r1 * s
        for d in range(3):
            sums[d + 1] = sums[d + 1] + (turned * unit[d] + r2 * v[d])
    return [x[:, :ATOMS] + x[:, ATOMS:] for x in sums]


def atom_kernel(
    feat, pos, nbr, cnt, rin, rout, mixes, head, updated, charge,
    mine, table, pos_pad, ask, ask_in, pos_in, part, part_in, send, recv, far_send, far_recv,
):
    a, b, c = lax.axis_index("gx"), lax.axis_index("gy"), lax.axis_index("gz")
    other = {"gz": 1 - c}
    barrier = pltpu.get_barrier_semaphore()

    def plane(da, db):
        return {"gx": lax.rem(a + da + GX, GX), "gy": lax.rem(b + db + GY, GY)}

    for da, db in PLANES:
        pl.semaphore_signal(barrier, inc=1, device_id=plane(da, db), device_id_type=BY_MESH)
    pl.semaphore_signal(barrier, inc=1, device_id=other, device_id_type=BY_MESH)

    own = feat[...].astype(F32).T
    mine[:256, :] = own.astype(BF16)
    pos_pad[...] = jnp.zeros_like(pos_pad)
    pos_pad[:3, :] = pos[...].astype(F32)
    mine[256:, :] = pos_pad[...].astype(BF16)
    ask[...] = jnp.zeros_like(ask)
    ask[:NEIGH, :] = nbr[...]
    ask[NEIGH : NEIGH + 1, :] = cnt[...]
    pl.semaphore_wait(barrier, len(PLANES) + 1)

    def far(source, target, i):
        return pltpu.make_async_remote_copy(
            source, target, far_send.at[i], far_recv.at[i], device_id=other, device_id_type=BY_MESH
        )

    asks = [far(ask, ask_in, 0), far(mine.at[256:], pos_in, 1)]
    for copy in asks:
        copy.start()
    copies = []
    for i, (da, db) in enumerate(PLANES):
        place = (1 - da) * 3 + (1 - db)
        copies.append(
            pltpu.make_async_remote_copy(
                mine,
                table.at[:, place * ATOMS : (place + 1) * ATOMS],
                send.at[i],
                recv.at[i],
                device_id=plane(da, db),
                device_id_type=BY_MESH,
            )
        )
    for copy in copies:
        copy.start()
    table[:, 4 * ATOMS : 5 * ATOMS] = mine[...]
    for copy in asks + copies:
        copy.wait()
    known = table[...]
    their = ask_in[...]
    sums = edge_sums(
        known, their[:NEIGH], their[NEIGH : NEIGH + 1], pos_in[...].astype(F32), False,
        rin[...], rout[...],
    )
    for i in range(4):
        part[i * CHAN : (i + 1) * CHAN, :] = sums[i].astype(BF16)
    partial = far(part, part_in, 2)
    partial.start()
    sums = edge_sums(
        known, nbr[...], cnt[...], pos_pad[...], True, rin[...], rout[...]
    )
    partial.wait()
    agg = [
        ((sums[i] + part_in[i * CHAN : (i + 1) * CHAN, :].astype(F32)) / NEIGH).astype(BF16)
        for i in range(4)
    ]
    mix = mixes[...]
    mixed = dot_nn(mix[: 2 * CHAN], agg[0])
    gate = 1.0 / (1.0 + jnp.exp(-mixed[CHAN:]))
    scalars = own[:CHAN] + silu(mixed[:CHAN])
    vectors = [
        own[CHAN * (d + 1) : CHAN * (d + 2)] + dot_nn(mix[2 * CHAN :], agg[d + 1]) * gate
        for d in range(3)
    ]
    result = jnp.concatenate([scalars] + vectors, axis=0).astype(BF16).astype(F32)
    updated[...] = result.T.astype(BF16)
    charge[...] = jnp.sum(head[...] * result[:CHAN], axis=0, keepdims=True)


def cell_rows(cells):
    p, q = cells[0], cells[1]
    return p * 40 + 8 * ((p * 43) >> 7) + q


def spread_kernel(cells, weight, charge, z_fwd, out, density):
    c = lax.axis_index("gz")
    density[...] = jnp.zeros_like(density)
    group = 8
    rows_iota = lax.broadcasted_iota(I32, (ROWS, ATOMS), 0)
    z_iota = lax.broadcasted_iota(I32, (ZPAD, ATOMS), 0)

    @pl.loop(0, SPLINE // group)
    def _(step):
        span = pl.ds(pl.multiple_of(step * group, group), group)
        place = cell_rows([cells[0, span, :], cells[1, span, :]])
        depth = cells[2, span, :]
        value = weight[span, :] * charge[...]
        pick = jnp.concatenate(
            [
                jnp.where(rows_iota == place[k : k + 1], 1.0, 0.0).astype(BF16)
                for k in range(group)
            ],
            axis=1,
        )
        spot = jnp.concatenate(
            [
                jnp.where(z_iota == depth[k : k + 1], value[k : k + 1], 0.0).astype(BF16)
                for k in range(group)
            ],
            axis=1,
        )
        density[...] += dot_nt(pick, spot)

    matrix = z_fwd[c]
    for g in range(5):
        block = density[g * 128 : (g + 1) * 128, :].astype(BF16)
        out[g, :, :] = dot_nt(matrix, block).astype(BF16)


def mesh_kernel(
    modes, y_mat, x_fwd, x_inv, order, back, z_inv, out,
    in1, out2, in2, out3, in3, out4, in4, send1, recv1, send2, recv2, send3, recv3, send4, recv4,
):
    a, b, c = lax.axis_index("gx"), lax.axis_index("gy"), lax.axis_index("gz")
    me = c * GY + b
    near, wide = GY * GZ, GX
    barrier = pltpu.get_barrier_semaphore()

    def near_id(i):
        return {"gy": lax.rem(i, GY), "gz": i // GY}

    @pl.loop(1, near)
    def _(d):
        pl.semaphore_signal(
            barrier, inc=1, device_id=near_id(lax.rem(me + d, near)), device_id_type=BY_MESH
        )

    @pl.loop(1, wide)
    def _(d):
        pl.semaphore_signal(
            barrier, inc=1, device_id={"gx": lax.rem(a + d, wide)}, device_id_type=BY_MESH
        )

    def tile(i, size):
        return pl.ds(pl.multiple_of(i * size, size), size)

    def exchange(count, here, source, target, send, recv, device):
        def copy(to, frm, i):
            return pltpu.make_async_remote_copy(
                source(to), target(frm), send.at[i], recv.at[frm],
                device_id=device(to), device_id_type=BY_MESH,
            )

        @pl.loop(1, count)
        def _(d):
            copy(lax.rem(here + d, count), here, d).start()

        target(here)[...] = source(here)[...]

        @pl.loop(1, count)
        def _(d):
            copy(lax.rem(here + d, count), lax.rem(here + d, count), d).wait_recv()

        @pl.loop(1, count)
        def _(d):
            copy(lax.rem(here + d, count), here, d).wait_send()

    def wide_id(i):
        return {"gx": i}

    signed = lambda i: jnp.where(i <= 128, i, i - 128).astype(F32)
    kz = me * 16 + a // 2
    ky = lax.rem(a, 2) * 128 + lax.broadcasted_iota(I32, (MESH, 128), 1)
    kx = lax.broadcasted_iota(I32, (MESH, 128), 0)
    fz = jnp.where(kz <= 128, kz, kz - 128).astype(F32)
    step_size = 2.0 * math.pi / MESH
    screen = 4.0 * math.pi / MESH
    fx, fy = signed(kx), signed(ky)
    ksquare = step_size * step_size * (fx * fx + fy * fy + fz * fz)
    green = jnp.exp(-0.5 * ksquare) / (ksquare + screen * screen)
    green = jnp.where((kx + ky + kz) == 0, 0.0, green)

    pl.semaphore_wait(barrier, near - 1 + wide - 1)

    exchange(
        near, me,
        lambda to: modes.at[:, tile(to, 16), :],
        lambda frm: in1.at[frm // GY, :, :, tile(lax.rem(frm, GY), 128)],
        send1, recv1, near_id,
    )
    matrix = y_mat[...]
    mixed = dot_nn(in1[0].reshape(80, 1024), matrix) + dot_nn(in1[1].reshape(80, 1024), matrix)
    stacked = jnp.concatenate(
        [mixed[:, i * MESH : (i + 1) * MESH].astype(BF16) for i in range(3)], axis=0
    )
    out2[...] = dot_nn(order[...], stacked).astype(BF16)

    def grid_tile(ref):
        return lambda i: ref.at[tile(i // 2, 16), tile(lax.rem(i, 2), 128)]

    def row_tile(ref):
        return lambda i: ref.at[tile(i, 16), :]

    exchange(wide, a, grid_tile(out2), row_tile(in2), send2, recv2, wide_id)
    spectrum = dot_nn(x_fwd[...], in2[...]) * green
    out3[...] = dot_nn(x_inv[...], spectrum.astype(BF16)).astype(BF16)
    exchange(wide, a, row_tile(out3), grid_tile(in3), send3, recv3, wide_id)
    stacked = dot_nn(back[...], in3[...]).astype(BF16)
    joined = jnp.concatenate([stacked[80 * i : 80 * (i + 1)] for i in range(3)], axis=1)
    out4[...] = dot_nt(joined, matrix).astype(BF16).reshape(5, 16, 1024)
    exchange(
        near, me,
        lambda to: out4.at[:, :, tile(lax.rem(to, GY), 128)],
        lambda frm: in4.at[:, tile(frm, 16), :],
        send4, recv4, near_id,
    )
    matrix = z_inv[c]
    for g in range(5):
        out[:, g * 128 : (g + 1) * 128] = dot_nn(matrix, in4[g]).astype(BF16)


def force_kernel(cells, slope, charge, potential, out, values):
    group = 8
    rows_iota = lax.broadcasted_iota(I32, (ROWS, ATOMS), 0)
    z_iota = lax.broadcasted_iota(I32, (ZPAD, ATOMS), 0)
    field = potential[...]

    @pl.loop(0, SPLINE // group)
    def _(step):
        span = pl.ds(pl.multiple_of(step * group, group), group)
        place = cell_rows([cells[0, span, :], cells[1, span, :]])
        depth = cells[2, span, :]
        pick = jnp.concatenate(
            [
                jnp.where(rows_iota == place[k : k + 1], 1.0, 0.0).astype(BF16)
                for k in range(group)
            ],
            axis=1,
        )
        lines = dot_nn(field, pick)
        values[span, :] = jnp.concatenate(
            [
                jnp.sum(
                    jnp.where(
                        z_iota == depth[k : k + 1], lines[:, k * ATOMS : (k + 1) * ATOMS], 0.0
                    ),
                    axis=0,
                    keepdims=True,
                )
                for k in range(group)
            ],
            axis=0,
        )

    found = values[...]
    for d in range(3):
        out[d : d + 1, :] = -charge[...] * jnp.sum(slope[d] * found, axis=0, keepdims=True)


LIMIT = 40 * 1024 * 1024
DMA = pltpu.SemaphoreType.DMA


def per_device(
    features, positions, neighbours, counts, cell_index, spline_weight, spline_slope,
    radial_in, radial_out, mix_scalar, mix_vector, mix_gate, charge_head,
):
    tab = tables()
    cells, weight, slope = cell_index[0, 0, 0], spline_weight[0, 0, 0], spline_slope[0, 0, 0]
    mixes = jnp.concatenate([mix_scalar.T, mix_gate.T, mix_vector.T], axis=0)
    updated, charge = pl.pallas_call(
        atom_kernel,
        out_shape=(
            jax.ShapeDtypeStruct((ATOMS, 4 * CHAN), BF16),
            jax.ShapeDtypeStruct((1, ATOMS), F32),
        ),
        in_specs=[VMEM] * 8,
        out_specs=(VMEM, VMEM),
        scratch_shapes=[
            pltpu.VMEM((272, ATOMS), BF16),
            pltpu.VMEM((272, 9 * ATOMS), BF16),
            pltpu.VMEM((16, ATOMS), F32),
            pltpu.VMEM((16, ATOMS), I32),
            pltpu.VMEM((16, ATOMS), I32),
            pltpu.VMEM((16, ATOMS), BF16),
            pltpu.VMEM((256, ATOMS), BF16),
            pltpu.VMEM((256, ATOMS), BF16),
            DMA((8,)),
            DMA((8,)),
            DMA((3,)),
            DMA((3,)),
        ],
        compiler_params=pltpu.CompilerParams(
            collective_id=0, has_side_effects=True, vmem_limit_bytes=LIMIT
        ),
        name="atoms",
    )(
        features[0, 0, 0], positions[0, 0, 0], neighbours[0, 0, 0], counts[0, 0],
        radial_in.T, radial_out.T, mixes, charge_head[:, None],
    )
    modes = pl.pallas_call(
        spread_kernel,
        out_shape=jax.ShapeDtypeStruct((5, MESH, 128), BF16),
        in_specs=[VMEM] * 4,
        out_specs=VMEM,
        scratch_shapes=[pltpu.VMEM((ROWS, ZPAD), F32)],
        compiler_params=pltpu.CompilerParams(vmem_limit_bytes=LIMIT),
        name="spread",
    )(cells, weight, charge, tab["z_fwd"])
    near, wide = GY * GZ, GX
    potential = pl.pallas_call(
        mesh_kernel,
        out_shape=jax.ShapeDtypeStruct((ZPAD, ROWS), BF16),
        in_specs=[VMEM] * 7,
        out_specs=VMEM,
        scratch_shapes=[
            pltpu.VMEM((2, 5, 16, 1024), BF16),
            pltpu.VMEM((256, 256), BF16),
            pltpu.VMEM((512, 128), BF16),
            pltpu.VMEM((512, 128), BF16),
            pltpu.VMEM((256, 256), BF16),
            pltpu.VMEM((5, 16, 1024), BF16),
            pltpu.VMEM((5, 256, 128), BF16),
            DMA((near,)), DMA((near,)), DMA((wide,)), DMA((wide,)),
            DMA((wide,)), DMA((wide,)), DMA((near,)), DMA((near,)),
        ],
        compiler_params=pltpu.CompilerParams(
            collective_id=1, has_side_effects=True, vmem_limit_bytes=LIMIT
        ),
        name="mesh",
    )(modes, tab["y"], tab["x_fwd"], tab["x_inv"], tab["order"], tab["back"], tab["z_inv"])
    forces = pl.pallas_call(
        force_kernel,
        out_shape=jax.ShapeDtypeStruct((3, ATOMS), F32),
        in_specs=[VMEM] * 4,
        out_specs=VMEM,
        scratch_shapes=[pltpu.VMEM((SPLINE, ATOMS), F32)],
        compiler_params=pltpu.CompilerParams(vmem_limit_bytes=LIMIT),
        name="forces",
    )(cells, slope, charge, potential)
    return (updated[None, None, None], forces[None, None, None])


def solution(mesh):
    placed = (
        P("gx", "gy", "gz", None, None),
        P("gx", "gy", "gz", None, None),
        P("gx", "gy", "gz", None, None),
        P("gx", "gy", "gz", None),
        P("gx", "gy", "gz", None, None, None),
        P("gx", "gy", "gz", None, None),
        P("gx", "gy", "gz", None, None, None),
        P(), P(), P(), P(), P(), P(),
    )
    return jax.shard_map(
        per_device,
        mesh=mesh,
        in_specs=placed,
        out_specs=(P("gx", "gy", "gz", None, None), P("gx", "gy", "gz", None, None)),
        check_vma=False,
    )
```

```python
import math

import jax
import jax.numpy as jnp
import numpy as np
from jax import lax
from jax.experimental import pallas as pl
from jax.experimental.pallas import tpu as pltpu
from jax.sharding import PartitionSpec as P

MESH = 256
GX, GY, GZ = 32, 8, 2
ATOMS, NEIGH, CHAN, SPLINE = 128, 12, 64, 64
F32, BF16, I32 = jnp.float32, jnp.bfloat16, jnp.int32
BY_MESH = pl.DeviceIdType.MESH
HIGHEST = lax.Precision.HIGHEST
VMEM = pl.BlockSpec(memory_space=pltpu.VMEM)
ANY = pl.BlockSpec(memory_space=pl.ANY)
PLANES = tuple((da, db) for da in (-1, 0, 1) for db in (-1, 0, 1) if (da, db) != (0, 0))
ZPAD = 136
ROWS = 640
GROUP = 8
CHUNKS = SPLINE // GROUP
WIDTH = GROUP * ATOMS


def real_basis():
    n = np.arange(MESH)[:, None]
    m = np.arange(MESH)[None, :]
    freq = np.where(m <= 128, m, m - 128)
    angle = 2.0 * np.pi * ((n * freq) % MESH) / MESH
    basis = np.where(m <= 128, np.cos(angle), np.sin(angle)) * np.sqrt(2.0 / MESH)
    basis[:, 0] = 1.0 / np.sqrt(MESH)
    basis[:, 128] /= np.sqrt(2.0)
    return basis


def tables():
    basis = real_basis()
    along_z = np.zeros((GZ, ZPAD, MESH))
    for c in range(GZ):
        along_z[c, :134] = basis[(128 * c + np.arange(134) - 3) % MESH]
    along_y = np.zeros((GY, 128, 3, MESH))
    for b in range(GY):
        for third in range(3):
            along_y[b, third * 40 : third * 40 + 38, third] = basis[
                (32 * b + np.arange(38) - 3) % MESH
            ]
    along_x = np.zeros((GX, 16, MESH))
    for a in range(GX):
        along_x[a, :14] = basis[(8 * a + np.arange(14) - 3) % MESH]
    order = np.zeros((16, 16, 3, 5, 16))
    for p in range(14):
        for k in range(16):
            order[k, p, p % 3, p // 3, k] = 1.0
    as_bf16 = lambda x: jnp.asarray(x, BF16)
    along_x = along_x.reshape(512, 256)
    order = order.reshape(256, 240)
    halves = along_z.reshape(GZ, ZPAD, 2, 128)
    return [
        as_bf16(halves.transpose(2, 0, 3, 1)),
        as_bf16(halves.transpose(2, 0, 1, 3)),
        as_bf16(along_y.reshape(1024, 768)),
        as_bf16(along_x.T),
        as_bf16(along_x),
        as_bf16(order),
        as_bf16(order.T),
    ]


def dot_nn(a, b, precision=None):
    return jnp.dot(a, b, preferred_element_type=F32, precision=precision)


def dot_nt(a, b):
    return lax.dot_general(a, b, (((1,), (1,)), ((), ())), preferred_element_type=F32)


def dot_tn(a, b):
    return lax.dot_general(a, b, (((0,), (0,)), ((), ())), preferred_element_type=F32)


def halves_of(x):
    high = x.astype(BF16).astype(F32)
    return high, x - high


def silu(x):
    return x / (1.0 + jnp.exp(-x))


def split_rows(rows):
    block = rows >> 7
    slot = rows & 127
    ninth = (block * 43) >> 7
    oz = block - 3 * ninth - 1
    third = (ninth * 43) >> 7
    ox = third - 1
    oy = ninth - 3 * third - 1
    return ninth * 128 + slot, ox, oy, oz


def fill_pick(pick, rows, counts, same_layer):
    index, ox, oy, oz = split_rows(rows)
    slot = lax.broadcasted_iota(I32, (NEIGH, ATOMS), 0)
    use = (oz == 0) if same_layer else (oz != 0)
    index = jnp.where(use & (slot < counts), index, -1)
    rows_iota = lax.broadcasted_iota(I32, (9 * ATOMS, ATOMS), 0)
    for k in range(NEIGH):
        pick[:, k * ATOMS : (k + 1) * ATOMS] = jnp.where(
            rows_iota == index[k : k + 1], 1.0, 0.0
        ).astype(BF16)
    return [8.0 * o.astype(F32) for o in (ox, oy, oz)]


def fill_radial(radial, units, pick, places, shift, own_pos, rin, rout):
    centre = 4.0 * lax.broadcasted_iota(I32, (8, 2 * ATOMS), 0).astype(F32)
    known = places[...]
    for pair in range(NEIGH // 2):
        ks = (2 * pair, 2 * pair + 1)
        span = slice(2 * pair * ATOMS, (2 * pair + 2) * ATOMS)
        got = dot_nn(known, pick[:, span])
        delta = []
        for d in range(3):
            moved = jnp.concatenate(
                [shift[d][k : k + 1] - own_pos[d : d + 1] for k in ks], axis=1
            )
            delta.append(got[d : d + 1] + moved)
        length = jnp.sqrt(delta[0] * delta[0] + delta[1] * delta[1] + delta[2] * delta[2] + 1.0)
        inverse = 1.0 / length
        for d in range(3):
            units[d : d + 1, span] = delta[d] * inverse
        off = length - centre
        high, low = halves_of(jnp.exp(off * off * -0.125))
        basis = jnp.concatenate([high, low, high, jnp.zeros_like(high)], axis=0).astype(BF16)
        high, low = halves_of(silu(dot_tn(rin, basis)))
        hidden = jnp.concatenate([high, low, high], axis=0).astype(BF16)
        radial[:, span] = dot_tn(rout, hidden)


def edge_sums(table, pick, radial, units):
    sums = [jnp.zeros((CHAN, 2 * ATOMS), F32) for _ in range(4)]
    known = table[...]
    for pair in range(NEIGH // 2):
        span = slice(2 * pair * ATOMS, (2 * pair + 2) * ATOMS)
        got = dot_nn(known, pick[:, span])
        r0 = radial[:CHAN, span]
        r1 = radial[CHAN : 2 * CHAN, span]
        r2 = radial[2 * CHAN :, span]
        unit = [units[d : d + 1, span] for d in range(3)]
        s = got[:CHAN]
        v = [got[CHAN * (d + 1) : CHAN * (d + 2)] for d in range(3)]
        along = unit[0] * v[0] + unit[1] * v[1] + unit[2] * v[2]
        sums[0] = sums[0] + (r0 * s + r2 * along)
        turned = r1 * s
        for d in range(3):
            sums[d + 1] = sums[d + 1] + (turned * unit[d] + r2 * v[d])
    return [x[:, :ATOMS] + x[:, ATOMS:] for x in sums]


def fill_cells(spots, cells):
    rows_iota = lax.broadcasted_iota(I32, (ROWS, ATOMS), 0)

    @pl.loop(0, CHUNKS)
    def _(step):
        span = pl.ds(pl.multiple_of(step * GROUP, GROUP), GROUP)
        p, q = cells[0, span, :], cells[1, span, :]
        place = p * 40 + 8 * ((p * 43) >> 7) + q
        for k in range(GROUP):
            spots[step, :, k * ATOMS : (k + 1) * ATOMS] = jnp.where(
                rows_iota == place[k : k + 1], 1.0, 0.0
            ).astype(BF16)


def spread(density, spots, cells, value):
    z_iota = lax.broadcasted_iota(I32, (ZPAD, ATOMS), 0)
    density[...] = jnp.zeros_like(density)

    @pl.loop(0, CHUNKS)
    def _(step):
        span = pl.ds(pl.multiple_of(step * GROUP, GROUP), GROUP)
        depth = cells[2, span, :]
        amount = value[span, :]
        lines = jnp.concatenate(
            [
                jnp.where(z_iota == depth[k : k + 1], amount[k : k + 1], 0.0).astype(BF16)
                for k in range(GROUP)
            ],
            axis=1,
        )
        density[...] += dot_nt(spots[step], lines)


def collect(values, spots, cells, field):
    z_iota = lax.broadcasted_iota(I32, (ZPAD, ATOMS), 0)

    @pl.loop(0, CHUNKS)
    def _(step):
        span = pl.ds(pl.multiple_of(step * GROUP, GROUP), GROUP)
        depth = cells[2, span, :]
        lines = dot_nn(field[...], spots[step])
        values[span, :] = jnp.concatenate(
            [
                jnp.sum(
                    jnp.where(
                        z_iota == depth[k : k + 1], lines[:, k * ATOMS : (k + 1) * ATOMS], 0.0
                    ),
                    axis=0,
                    keepdims=True,
                )
                for k in range(GROUP)
            ],
            axis=0,
        )


def tile(i, size):
    return pl.ds(pl.multiple_of(i * size, size), size)


def signed(i):
    return jnp.where(i <= 128, i, i - 128).astype(F32)


class Exchange:
    def __init__(self, count, here, source, target, send, recv, device):
        self.count, self.here, self.source, self.target = count, here, source, target
        self.send, self.recv, self.device = send, recv, device

    def copy(self, to, frm, i):
        return pltpu.make_async_remote_copy(
            self.source(to), self.target(frm), self.send.at[i], self.recv.at[frm],
            device_id=self.device(to), device_id_type=BY_MESH,
        )

    def run(self):
        count, here = self.count, self.here

        @pl.loop(1, count)
        def _(d):
            self.copy(lax.rem(here + d, count), here, d).start()

        self.target(here)[...] = self.source(here)[...]

        @pl.loop(1, count)
        def _(d):
            frm = lax.rem(here + d, count)
            self.copy(frm, frm, d).wait_recv()

    def finish(self):
        @pl.loop(1, self.count)
        def _(d):
            self.copy(lax.rem(self.here + d, self.count), self.here, d).wait_send()


def whole_kernel(
    feat, pos, nbr, cnt, cells_in, weight_in, slope_in, rin_in, rout_in, mix_s_in, mix_v_in,
    mix_g_in, head, *rest,
):
    consts_in, rest = rest[:7], rest[7:]
    (updated, forces), rest = rest[:2], rest[2:]
    loads, rest = rest[:16], rest[16:]
    (
        own_feat, rows_in, cells, weight, slope, rin_v, rout_v, mix_s, mix_v, mix_g
    ) = loads[:9] + loads[9:10]
    z_fwd, z_inv, y_mat, x_fwd, x_inv, order = loads[10:16]
    (
        back, load_sem, mine, table, places, pos_pad, ask, ask_in, pos_in, own_in, part, part_in,
        same, same_in, points, points_in, cells_par, pick_own, pick_par, radial_own, radial_par,
        units_own, units_par, spots_own, spots_par, value, density_own, density_par, modes, in1,
        out2, in2, out3, in3, out4, in4, field, values, force, force_in,
        pos_send, pos_recv, send, recv, far_send, far_recv,
        send1, recv1, send2, recv2, send3, recv3, send4, recv4,
    ) = rest
    a, b, c = lax.axis_index("gx"), lax.axis_index("gy"), lax.axis_index("gz")
    other = {"gz": 1 - c}
    barrier = pltpu.get_barrier_semaphore()

    inputs = [feat, nbr, cells_in, weight_in, slope_in, rin_in, rout_in, mix_s_in, mix_v_in, mix_g_in]
    fetch = [
        pltpu.make_async_copy(source, target, load_sem.at[i])
        for i, (source, target) in enumerate(
            zip(inputs + list(consts_in), list(loads) + [back])
        )
    ]
    for copy in fetch:
        copy.start()

    def plane(da, db):
        return {"gx": lax.rem(a + da + GX, GX), "gy": lax.rem(b + db + GY, GY)}

    def gy_id(i):
        return {"gy": i}

    def gx_id(i):
        return {"gx": i}

    def greet(device):
        pl.semaphore_signal(barrier, inc=1, device_id=device, device_id_type=BY_MESH)

    greet(other)
    for da, db in PLANES:
        if da and db:
            greet(plane(da, db))

    @pl.loop(1, GX)
    def _(d):
        greet(gx_id(lax.rem(a + d, GX)))

    @pl.loop(1, GY)
    def _(d):
        greet(gy_id(lax.rem(b + d, GY)))

    fetch[0].wait()
    own = own_feat[...].astype(F32).T
    mine[...] = own.astype(BF16)
    pos_pad[...] = jnp.zeros_like(pos_pad)
    pos_pad[:3, :] = pos[...].astype(F32)
    own_pos16 = pos_pad[...].astype(BF16)
    places[:, 4 * ATOMS : 5 * ATOMS] = own_pos16
    table[:, 4 * ATOMS : 5 * ATOMS] = mine[...]
    fetch[1].wait()
    ask[...] = jnp.zeros_like(ask)
    for k in range(NEIGH):
        ask[k : k + 1, :] = rows_in[k]
    ask[NEIGH : NEIGH + 1, :] = cnt[...]
    for copy in fetch[2:5]:
        copy.wait()
    for d in range(3):
        points[d] = cells[d].astype(F32).astype(BF16)
        points[4 + d] = slope[d].astype(BF16)
    points[3] = weight[...].astype(BF16)
    for copy in fetch[5:]:
        copy.wait()
    high, low = halves_of(rin_v[...])
    rin = jnp.concatenate([high, high, low, jnp.zeros_like(high)], axis=0).astype(BF16)
    high, low = halves_of(rout_v[...])
    rout = jnp.concatenate([high, high, low], axis=0).astype(BF16)

    pl.semaphore_wait(barrier, 1 + 4 + GX - 1 + GY - 1)

    def far(source, target, i):
        return pltpu.make_async_remote_copy(
            source, target, far_send.at[i], far_recv.at[i], device_id=other, device_id_type=BY_MESH
        )

    center = slice(4 * ATOMS, 5 * ATOMS)
    asks = [far(ask, ask_in, 0), far(places.at[:, center], pos_in, 1)]
    for copy in asks:
        copy.start()
    spot_copies, copies = [], []
    for i, (da, db) in enumerate(PLANES):
        place = (1 - da) * 3 + (1 - db)
        span = slice(place * ATOMS, (place + 1) * ATOMS)
        for group, source, target, s, r in (
            (spot_copies, places.at[:, center], places.at[:, span], pos_send, pos_recv),
            (copies, mine, table.at[:, span], send, recv),
        ):
            group.append(
                pltpu.make_async_remote_copy(
                    source, target, s.at[i], r.at[i], device_id=plane(da, db), device_id_type=BY_MESH
                )
            )
    for copy in spot_copies + copies:
        copy.start()
    scalars_far = far(mine.at[:CHAN], own_in, 2)
    scalars_far.start()
    points_far = far(points, points_in, 3)
    points_far.start()

    shift_own = fill_pick(pick_own, ask[:NEIGH], ask[NEIGH : NEIGH + 1], True)
    fill_cells(spots_own, cells)
    for copy in asks + spot_copies:
        copy.wait_recv()
    shift_par = fill_pick(pick_par, ask_in[:NEIGH], ask_in[NEIGH : NEIGH + 1], False)
    fill_radial(
        radial_par, units_par, pick_par, places, shift_par, pos_in[...].astype(F32), rin, rout
    )
    fill_radial(radial_own, units_own, pick_own, places, shift_own, pos_pad[...], rin, rout)
    for copy in copies:
        copy.wait_recv()
    sums = edge_sums(table, pick_par, radial_par, units_par)
    for i in range(4):
        part[i * CHAN : (i + 1) * CHAN, :] = sums[i].astype(BF16)
    partial = far(part, part_in, 4)
    partial.start()
    sums = edge_sums(table, pick_own, radial_own, units_own)
    same[...] = sums[0].astype(BF16)
    same_far = far(same, same_in, 5)
    same_far.start()
    points_far.wait_recv()
    for d in range(3):
        cells_par[d] = points_in[d].astype(F32).astype(I32)
    fill_cells(spots_par, cells_par)

    kz = c * 128 + b * 16 + a // 2
    ky = lax.rem(a, 2) * 128 + lax.broadcasted_iota(I32, (MESH, 128), 1)
    kx = lax.broadcasted_iota(I32, (MESH, 128), 0)
    fz = jnp.where(kz <= 128, kz, kz - 128).astype(F32)
    step_size = 2.0 * math.pi / MESH
    screen = 4.0 * math.pi / MESH
    fx, fy = signed(kx), signed(ky)
    ksquare = step_size * step_size * (fx * fx + fy * fy + fz * fz)
    green = jnp.exp(-0.5 * ksquare) / (ksquare + screen * screen)
    green = jnp.where((kx + ky + kz) == 0, 0.0, green)

    scalars_far.wait_recv()
    same_far.wait_recv()
    partial.wait_recv()

    def gather_sum(layer, far_part):
        return ((layer.astype(F32) + far_part.astype(F32)) / NEIGH).astype(BF16)

    head_row = head[...]

    def charge_of(scalars):
        high, low = halves_of(head_row)
        rows = jnp.concatenate([high, low, low - low.astype(BF16).astype(F32)], axis=0)
        return jnp.sum(dot_nn(rows.astype(BF16), scalars), axis=0, keepdims=True)

    agg_s = gather_sum(same[...], part_in[:CHAN, :])
    agg_par = gather_sum(same_in[...], part[:CHAN, :])
    scalars = (own[:CHAN] + silu(dot_tn(mix_s[...], agg_s))).astype(BF16)
    scalars_par = (
        own_in[...].astype(F32) + silu(dot_tn(mix_s[...], agg_par))
    ).astype(BF16)
    charge = charge_of(scalars)
    charge_par = charge_of(scalars_par)

    value[...] = weight[...] * charge
    spread(density_own, spots_own, cells, value)
    value[...] = points_in[3].astype(F32) * charge_par
    spread(density_par, spots_par, cells_par, value)
    fwd_own, fwd_par = z_fwd[c, c], z_fwd[c, 1 - c]
    for g in range(5):
        span = slice(g * 128, (g + 1) * 128)
        modes[g, :, :] = (
            dot_nt(fwd_own, density_own[span, :].astype(BF16))
            + dot_nt(fwd_par, density_par[span, :].astype(BF16))
        ).astype(BF16)

    def grid_tile(ref):
        return lambda i: ref.at[tile(i // 2, 16), tile(lax.rem(i, 2), 128)]

    def row_tile(ref):
        return lambda i: ref.at[tile(i, 16), :]

    def mid_tile(ref):
        return lambda i: ref.at[:, tile(i, 16), :]

    def lane_tile(ref):
        return lambda i: ref.at[:, :, tile(i, 128)]

    first = Exchange(GY, b, mid_tile(modes), lane_tile(in1), send1, recv1, gy_id)
    second = Exchange(GX, a, grid_tile(out2), row_tile(in2), send2, recv2, gx_id)
    third = Exchange(GX, a, row_tile(out3), grid_tile(in3), send3, recv3, gx_id)
    fourth = Exchange(GY, b, lane_tile(out4), mid_tile(in4), send4, recv4, gy_id)

    first.run()
    mixed = dot_nn(in1[...].reshape(80, 1024), y_mat[...])
    stacked = jnp.concatenate(
        [mixed[:, i * MESH : (i + 1) * MESH].astype(BF16) for i in range(3)], axis=0
    )
    out2[...] = dot_nn(order[...], stacked).astype(BF16)
    second.run()
    spectrum = dot_nn(x_fwd[...], in2[...]) * green
    out3[...] = dot_nn(x_inv[...], spectrum.astype(BF16)).astype(BF16)
    third.run()
    stacked = dot_nn(back[...], in3[...]).astype(BF16)
    joined = jnp.concatenate([stacked[80 * i : 80 * (i + 1)] for i in range(3)], axis=1)
    out4[...] = dot_nt(joined, y_mat[...]).astype(BF16).reshape(5, 16, 1024)
    fourth.run()

    def potential(matrix):
        for g in range(5):
            field[:, g * 128 : (g + 1) * 128] = dot_nn(matrix, in4[g]).astype(BF16)

    potential(z_inv[c, 1 - c])
    collect(values, spots_par, cells_par, field)
    found = values[...]
    for d in range(3):
        force[d : d + 1, :] = jnp.sum(
            points_in[4 + d].astype(F32) * found, axis=0, keepdims=True
        )
    force[3:, :] = jnp.zeros((5, ATOMS), F32)
    forces_far = far(force, force_in, 6)
    forces_far.start()
    potential(z_inv[c, c])
    collect(values, spots_own, cells, field)
    found = values[...]
    totals = [jnp.sum(slope[d] * found, axis=0, keepdims=True) for d in range(3)]

    agg_v = [
        gather_sum(sums[d + 1], part_in[(d + 1) * CHAN : (d + 2) * CHAN, :]) for d in range(3)
    ]
    gate = 1.0 / (1.0 + jnp.exp(-dot_tn(mix_g[...], agg_s)))
    vectors = [
        own[CHAN * (d + 1) : CHAN * (d + 2)] + dot_tn(mix_v[...], agg_v[d]) * gate
        for d in range(3)
    ]
    result = jnp.concatenate([scalars.astype(F32)] + vectors, axis=0)
    updated[...] = result.T.astype(BF16)
    for copy in asks + spot_copies + copies + [scalars_far, points_far, partial, same_far]:
        copy.wait_send()
    for step in (first, second, third, fourth):
        step.finish()
    forces_far.wait()
    for d in range(3):
        forces[d] = -charge * (totals[d] + force_in[d : d + 1, :])


LIMIT = 60 * 1024 * 1024
DMA = pltpu.SemaphoreType.DMA


def per_device(
    features, positions, neighbours, counts, cell_index, spline_weight, spline_slope,
    radial_in, radial_out, mix_scalar, mix_vector, mix_gate, charge_head,
):
    consts = tables()
    inputs = [
        features[0, 0, 0], positions[0, 0, 0], neighbours.reshape(NEIGH, 1, ATOMS), counts[0, 0],
        cell_index[0, 0, 0], spline_weight[0, 0, 0], spline_slope[0, 0, 0],
        radial_in, radial_out, mix_scalar, mix_vector, mix_gate, charge_head[None, :],
    ] + consts
    fetched = [inputs[i] for i in (0, 2, 4, 5, 6, 7, 8, 9, 10, 11)] + consts
    edges = NEIGH * ATOMS
    buffer = lambda shape, dtype: pltpu.VMEM(shape, dtype)
    updated, forces = pl.pallas_call(
        whole_kernel,
        out_shape=(
            jax.ShapeDtypeStruct((ATOMS, 4 * CHAN), BF16),
            jax.ShapeDtypeStruct((3, 1, ATOMS), F32),
        ),
        in_specs=[ANY, VMEM, ANY, VMEM] + [ANY] * 8 + [VMEM] + [ANY] * 7,
        out_specs=(VMEM, VMEM),
        scratch_shapes=[buffer(x.shape, x.dtype) for x in fetched]
        + [
            DMA((17,)),
            buffer((256, ATOMS), BF16),
            buffer((256, 9 * ATOMS), BF16),
            buffer((16, 9 * ATOMS), BF16),
            buffer((16, ATOMS), F32),
            buffer((16, ATOMS), I32),
            buffer((16, ATOMS), I32),
            buffer((16, ATOMS), BF16),
            buffer((CHAN, ATOMS), BF16),
            buffer((256, ATOMS), BF16),
            buffer((256, ATOMS), BF16),
            buffer((CHAN, ATOMS), BF16),
            buffer((CHAN, ATOMS), BF16),
            buffer((7, SPLINE, ATOMS), BF16),
            buffer((7, SPLINE, ATOMS), BF16),
            buffer((3, SPLINE, ATOMS), I32),
            buffer((9 * ATOMS, edges), BF16),
            buffer((9 * ATOMS, edges), BF16),
            buffer((3 * CHAN, edges), F32),
            buffer((3 * CHAN, edges), F32),
            buffer((8, edges), F32),
            buffer((8, edges), F32),
            buffer((CHUNKS, ROWS, WIDTH), BF16),
            buffer((CHUNKS, ROWS, WIDTH), BF16),
            buffer((SPLINE, ATOMS), F32),
            buffer((ROWS, ZPAD), F32),
            buffer((ROWS, ZPAD), F32),
            buffer((5, 128, 128), BF16),
            buffer((5, 16, 1024), BF16),
            buffer((256, 256), BF16),
            buffer((512, 128), BF16),
            buffer((512, 128), BF16),
            buffer((256, 256), BF16),
            buffer((5, 16, 1024), BF16),
            buffer((5, 128, 128), BF16),
            buffer((ZPAD, ROWS), BF16),
            buffer((SPLINE, ATOMS), F32),
            buffer((8, ATOMS), F32),
            buffer((8, ATOMS), F32),
            DMA((8,)), DMA((8,)), DMA((8,)), DMA((8,)), DMA((7,)), DMA((7,)),
            DMA((GY,)), DMA((GY,)), DMA((GX,)), DMA((GX,)),
            DMA((GX,)), DMA((GX,)), DMA((GY,)), DMA((GY,)),
        ],
        compiler_params=pltpu.CompilerParams(
            collective_id=0, has_side_effects=True, vmem_limit_bytes=LIMIT
        ),
        name="whole",
    )(*inputs)
    return (updated[None, None, None], forces.reshape(1, 1, 1, 3, ATOMS))


def solution(mesh):
    placed = (
        P("gx", "gy", "gz", None, None),
        P("gx", "gy", "gz", None, None),
        P("gx", "gy", "gz", None, None),
        P("gx", "gy", "gz", None),
        P("gx", "gy", "gz", None, None, None),
        P("gx", "gy", "gz", None, None),
        P("gx", "gy", "gz", None, None, None),
        P(), P(), P(), P(), P(), P(),
    )
    return jax.shard_map(
        per_device,
        mesh=mesh,
        in_specs=placed,
        out_specs=(P("gx", "gy", "gz", None, None), P("gx", "gy", "gz", None, None)),
        check_vma=False,
    )
```
